32 devices in a mesh: group: 2 (over x), tm: 16 (over z, y, core).
Axes of the slice: x: 2, y: 2, z: 4, core: 2. Of those that a mesh axis runs over, the one named last changes fastest.
Arguments:
- queries: bfloat16 [8192, 1536], P(('group', 'tm')), parts along dimension 0, may hold values from -7 to 7, as said below
- keys: bfloat16 [8192, 1536], P(('group', 'tm')), parts along dimension 0, may hold values from -6 to 6, as said below
- values: bfloat16 [8192, 1536], P(('group', 'tm')), parts along dimension 0, may hold values from -6 to 6
- grad_out: bfloat16 [8192, 1536], P(('group', 'tm')), parts along dimension 0, may hold values from -96 to 96
- block_list: int32 [128, 30], P(('group', 'tm')), parts along dimension 0, may hold values 0 or 1
Outputs:
- grad_queries: bfloat16 [8192, 1536], P(('group', 'tm')), parts along dimension 0
- grad_keys: bfloat16 [8192, 1536], P(('group', 'tm')), parts along dimension 0
- grad_values: bfloat16 [8192, 1536], P(('group', 'tm')), parts along dimension 0
The draws below stay inside these ranges and needn't reach their ends.
There are 2 independent parts, one for each index of `group`. The reference program is written for one: setup_inputs(seed, part) draws one part's arguments, and reference() takes and returns one part's arrays. A program takes and returns all parts, laid end to end along the dimension named above; each array names one. Nothing has to cross between parts.
Inputs may be any that keep to these rules, and one draw needn't show every extreme that they name: `queries`: entries of order one. `keys`: entries of order one. `block_list`: columns follow the candidate order of the steps.
All inputs are finite; a program needn't handle non-finite values. No bound on the sum of `block_list` on one device may be relied on, other than what follows from the above.
Results may differ from the reference program's by a relative error of at most 0.0073.
Values may be sent and summed in bfloat16 or wider, within the bound.
A program may use at most 128 MiB of HBM per device.

```python
import jax
import jax.numpy as jnp
import numpy as np
from jax import lax

HEADS = 12
HDIM = 128
BLOCK = 64
REACH = 2
FRAMES = 2
BANDS = 2
TOKENS = 4096
QBLOCKS = 64
CANDS = 30
N_TM = 16


def draw_pair(key):
    base = jax.random.fold_in(key, 11)
    key_query, key_key = jax.random.split(base, 2)
    width = HEADS * HDIM
    query_vals = jnp.clip(jax.random.normal(key_query, (TOKENS, width), jnp.float32), -6.0, 6.0)
    key_vals = jnp.clip(jax.random.normal(key_key, (TOKENS, width), jnp.float32), -6.0, 6.0)
    return (query_vals, key_vals)


def draw_queries(key, part):
    return draw_pair(key)[0].astype(jnp.bfloat16)


def draw_keys(key, part):
    return draw_pair(key)[1].astype(jnp.bfloat16)


def with_ends(entries, rng, smallest, high):
    spot = [jax.random.randint(jax.random.fold_in(rng, axis), (), 0, length) for axis, length in enumerate(entries.shape)]
    main_axis = entries.shape.index(max(entries.shape))
    beside = spot[:main_axis] + [(spot[main_axis] + 1) % entries.shape[main_axis]] + spot[main_axis + 1:]
    return entries.at[tuple(spot)].set(smallest).at[tuple(beside)].set(high)


def block_levels(rng, extent, cuts, low, top_value):
    level, own = 1.0, jax.random.fold_in(rng, 6)
    for dim, blocks in cuts:
        heights = jnp.exp(jax.random.uniform(jax.random.fold_in(own, dim), (blocks,), jnp.float32, low / len(cuts), top_value / len(cuts)))
        level = level * jnp.repeat(heights, extent[dim] // blocks).reshape([-1 if axis == dim else 1 for axis in range(len(extent))])
    return level


def gaussian(rng, shape, scale, most, pieces=(), kind=jnp.bfloat16):
    result = jax.random.normal(rng, shape, jnp.float32) * scale
    if len(pieces) > 0:
        result = block_levels(rng, shape, pieces, -0.22, 0.18) * result
    return jnp.clip(result, min=-most, max=most).astype(kind)


def setup_inputs(seed: int = 0, part: int = 0) -> dict:
    arg_keys = jax.random.split(jax.random.key(seed), 6)
    part_splits = jax.random.split(jax.random.fold_in(arg_keys[5], part), 6)
    return {
        "queries": draw_queries(jax.random.fold_in(jax.random.fold_in(arg_keys[5], part), 71), part),
        "keys": draw_keys(jax.random.fold_in(jax.random.fold_in(arg_keys[5], part), 71), part),
        "values": gaussian(part_splits[2], (TOKENS, HEADS * HDIM), 1.0, 6.0, ((0, 16),)),
        "grad_out": gaussian(part_splits[3], (TOKENS, HEADS * HDIM), 16.0, 96.0, ((0, 16),)),
        "block_list": with_ends((jax.random.randint(part_splits[4], (QBLOCKS, CANDS), 0, 3) < 2).astype(jnp.int32), jax.random.fold_in(part_splits[4], 1), 0, 1),
    }


def settle(tensor):
    return lax.optimization_barrier(tensor.astype(jnp.bfloat16)).astype(jnp.float32)


def pair_tables(slots):
    blocks_group = FRAMES * BANDS
    query_block = np.arange(blocks_group)[:, None]
    key_block = np.arange(slots * blocks_group)[None, :]
    slot_of = key_block // blocks_group
    frame_key = (key_block // BANDS) % FRAMES
    band_key = key_block % BANDS
    frame_query = query_block // BANDS
    band_query = query_block % BANDS
    cand = (slot_of * FRAMES + frame_key) * 3 + band_key - band_query + 1
    own_block = (slot_of == REACH) & (frame_key == frame_query) & (band_key == band_query)
    cand = cand + 0 * query_block
    slot_full = slot_of + 0 * query_block
    return cand, own_block, slot_full


def listed_mask(block_rows, group_index, groups):
    slots = 2 * REACH + 1
    cand, own_block, slot_full = pair_tables(slots)
    chosen = (block_rows > 0)[np.arange(FRAMES * BANDS)[:, None], cand]
    group_pos = group_index + jnp.asarray(slot_full, jnp.int32) - REACH
    group_ok = (group_pos >= 0) & (group_pos < groups)
    allowed = (chosen & group_ok) | jnp.asarray(own_block)
    return allowed[:, None, :, None]


def group_grads(query_rows, grad_rows, key_window, value_window, block_rows, group_index, groups):
    scaling = HDIM ** -0.5
    allowed = listed_mask(block_rows, group_index, groups)
    slots = key_window.shape[0]
    tok_dev = FRAMES * BANDS * BLOCK
    width = HEADS * HDIM
    key_flat = key_window.reshape(slots * tok_dev, width)
    value_flat = value_window.reshape(slots * tok_dev, width)
    query_list, key_list, value_list = [], [], []
    for head_index in range(HEADS):
        cols = slice(head_index * HDIM, (head_index + 1) * HDIM)
        query_head = query_rows[:, cols].astype(jnp.float32)
        grad_head = grad_rows[:, cols].astype(jnp.float32)
        key_head = key_flat[:, cols].astype(jnp.float32)
        value_head = value_flat[:, cols].astype(jnp.float32)
        scores = jnp.einsum('qd,kd->qk', query_head, key_head) * scaling
        shaped = jnp.where(allowed, scores.reshape(FRAMES * BANDS, BLOCK, slots * FRAMES * BANDS, BLOCK), -jnp.inf)
        row_max = jnp.max(shaped, axis=(2, 3), keepdims=True)
        log_total = row_max + jnp.log(jnp.sum(jnp.exp(shaped - row_max), axis=(2, 3), keepdims=True))
        weights = jnp.exp(shaped - log_total).reshape(scores.shape)
        weights_low = settle(weights)
        attended = jnp.einsum('qk,kd->qd', weights_low, value_head)
        deltas = jnp.sum(grad_head * attended, axis=-1, keepdims=True)
        grad_probs = jnp.einsum('qd,kd->qk', grad_head, value_head)
        grad_scores = settle(weights * (grad_probs - deltas))
        query_list.append(jnp.einsum('qk,kd->qd', grad_scores, key_head) * scaling)
        key_list.append((jnp.einsum('qk,qd->kd', grad_scores, query_head) * scaling).reshape(slots, tok_dev, HDIM))
        value_list.append(jnp.einsum('qk,qd->kd', weights_low, grad_head).reshape(slots, tok_dev, HDIM))
    return jnp.concatenate(query_list, axis=-1), jnp.concatenate(key_list, axis=-1), jnp.concatenate(value_list, axis=-1)


def reference(queries, keys, values, grad_out, block_list):
    groups = N_TM
    tok_dev = FRAMES * BANDS * BLOCK
    width = HEADS * HDIM
    slots = 2 * REACH + 1
    key_pad = jnp.pad(keys.reshape(groups, tok_dev, width), ((REACH, REACH), (0, 0), (0, 0)))
    value_pad = jnp.pad(values.reshape(groups, tok_dev, width), ((REACH, REACH), (0, 0), (0, 0)))
    query_groups = queries.reshape(groups, tok_dev, width)
    grad_groups = grad_out.reshape(groups, tok_dev, width)
    list_groups = block_list.reshape(groups, FRAMES * BANDS, CANDS)

    def visit_group(totals, inputs):
        key_total, value_total = totals
        query_rows, grad_rows, block_rows, group_index = inputs
        key_window = lax.dynamic_slice_in_dim(key_pad, group_index, slots, 0)
        value_window = lax.dynamic_slice_in_dim(value_pad, group_index, slots, 0)
        query_grad, key_grad, value_grad = group_grads(query_rows, grad_rows, key_window, value_window, block_rows, group_index, groups)
        key_now = lax.dynamic_slice_in_dim(key_total, group_index, slots, 0) + settle(key_grad)
        value_now = lax.dynamic_slice_in_dim(value_total, group_index, slots, 0) + settle(value_grad)
        key_total = lax.dynamic_update_slice_in_dim(key_total, key_now, group_index, 0)
        value_total = lax.dynamic_update_slice_in_dim(value_total, value_now, group_index, 0)
        return (key_total, value_total), query_grad.astype(jnp.bfloat16)

    zeros_acc = jnp.zeros((groups + 2 * REACH, tok_dev, width), jnp.float32)
    (key_total, value_total), query_grads = lax.scan(visit_group, (zeros_acc, zeros_acc), (query_groups, grad_groups, list_groups, jnp.arange(groups, dtype=jnp.int32)))
    grad_queries = query_grads.reshape(TOKENS, width)
    grad_keys = key_total[REACH:REACH + groups].reshape(TOKENS, width).astype(jnp.bfloat16)
    grad_values = value_total[REACH:REACH + groups].reshape(TOKENS, width).astype(jnp.bfloat16)
    return (grad_queries, grad_keys, grad_values)
```

```python
import functools
import math

import jax
import jax.numpy as jnp
from jax import lax
from jax.experimental import pallas as pl
from jax.experimental.pallas import tpu as pltpu
from jax.sharding import PartitionSpec as P

HDIM = 128
BLOCK = 64
REACH = 2
FRAMES = 2
BANDS = 2
SLOTS = 2 * REACH + 1
BLOCKS = FRAMES * BANDS
TOK = BLOCKS * BLOCK
MESH = pl.DeviceIdType.MESH
AHEAD = 12

OWN, SIB, PARTNER, EXTRA, RELAY = range(5)


def place(tm_count):
    here = lax.axis_index("tm")
    core = lax.rem(here, 2)
    half = lax.rem(here // 2, 2)
    column = here // 4
    columns = tm_count // 4
    down, up = column > 0, column < columns - 1
    even = half == 0
    has_relay = (even & down) | (~even & up)
    has_target = (even & up) | (~even & down)
    return here, core, half, down, up, has_relay, has_target


def slot_bias(block_list, tm_count):
    here, core, half, _, _, _, _ = place(tm_count)
    shape = (SLOTS * BLOCKS, BLOCKS, FRAMES * SLOTS * 3)
    key_block = lax.broadcasted_iota(jnp.int32, shape, 0)
    query_block = lax.broadcasted_iota(jnp.int32, shape, 1)
    slot = key_block // BLOCKS
    offset = jnp.where(
        slot == OWN, REACH,
        jnp.where(
            slot == SIB, 3 - 2 * core,
            jnp.where(
                slot == PARTNER, 4 - 4 * half,
                jnp.where(slot == EXTRA, 1 + 2 * core, 4 * half),
            ),
        ),
    )
    frame = key_block // BANDS % FRAMES
    band = key_block % BANDS
    cand = (offset * FRAMES + frame) * 3 + band - query_block % BANDS + 1
    group = here + offset - REACH
    exists = (group >= 0) & (group < tm_count)
    hit = exists & (lax.broadcasted_iota(jnp.int32, shape, 2) == cand)
    mine = (slot == OWN) & (key_block % BLOCKS == query_block)
    hits = (hit & (block_list > 0)[None]) | mine
    listed = jnp.max(hits.astype(jnp.float32), axis=2, keepdims=True)
    listed = jnp.broadcast_to(listed, (SLOTS * BLOCKS, BLOCKS, BLOCK))
    return jnp.where(listed > 0.5, 0.0, -jnp.inf).reshape(SLOTS * BLOCKS, TOK)


def kernel(
    tm_count, heads,
    q_ref, k_ref, v_ref, do_ref, bias_ref,
    dq_ref, dk_ref, dv_ref,
    kv, back_out, back_in, own_acc, partner_acc, relay_acc,
    fwd_send, fwd_recv, back_send, back_recv,
):
    here, core, half, down, up, has_relay, has_target = place(tm_count)
    sibling = here + 1 - 2 * core
    partner = here + 2 - 4 * half
    target = here + 4 - 8 * half
    source = here - 4 + 8 * half
    same = half == core
    scale = HDIM ** -0.5
    scale2 = scale * math.log2(math.e)

    barrier = pltpu.get_barrier_semaphore()

    def greet(device):
        pl.semaphore_signal(barrier, inc=1, device_id={"tm": device}, device_id_type=MESH)

    greet(sibling)
    greet(partner)

    @pl.when(down)
    def _():
        greet(here - 4)

    @pl.when(up)
    def _():
        greet(here + 4)

    def columns(h):
        return pl.ds(pl.multiple_of(h * HDIM, HDIM), HDIM)

    def pack(h, carry):
        kv[OWN, h, 0:TOK, :] = k_ref[:, columns(h)]
        kv[OWN, h, TOK:2 * TOK, :] = v_ref[:, columns(h)]
        return carry

    lax.fori_loop(0, heads, pack, 0)

    @pl.when(~has_relay)
    def _():
        def clear(h, carry):
            kv[RELAY, h] = jnp.zeros((2 * TOK, HDIM), jnp.bfloat16)
            return carry

        lax.fori_loop(0, heads, clear, 0)

    @pl.when(same & ~has_relay)
    def _():
        def clear(h, carry):
            kv[EXTRA, h] = jnp.zeros((2 * TOK, HDIM), jnp.bfloat16)
            return carry

        lax.fori_loop(0, heads, clear, 0)

    pl.semaphore_wait(barrier, 2 + down.astype(jnp.int32) + up.astype(jnp.int32))

    def forward(slot_from, slot_to, h, device):
        return pltpu.make_async_remote_copy(
            src_ref=kv.at[slot_from, h],
            dst_ref=kv.at[slot_to, h],
            send_sem=fwd_send.at[slot_to - 1, h],
            recv_sem=fwd_recv.at[slot_to - 1, h],
            device_id={"tm": device},
            device_id_type=MESH,
        )

    def backward(slot, h, device):
        return pltpu.make_async_remote_copy(
            src_ref=back_out.at[slot - 1, h],
            dst_ref=back_in.at[slot - 1, h],
            send_sem=back_send.at[slot - 1, h],
            recv_sem=back_recv.at[slot - 1, h],
            device_id={"tm": device},
            device_id_type=MESH,
        )

    def send_own(h):
        forward(OWN, PARTNER, h, partner).start()
        forward(OWN, SIB, h, sibling).start()

    def first(h, carry):
        send_own(h)
        return carry

    lax.fori_loop(0, min(AHEAD, heads), first, 0)

    def pass_partner(h):
        forward(OWN, PARTNER, h, partner).wait_recv()

        @pl.when(has_target)
        def _():
            forward(PARTNER, RELAY, h, target).start()

        @pl.when(same)
        def _():
            forward(PARTNER, EXTRA, h, sibling).start()

    def pass_relay(h):
        @pl.when(has_relay)
        def _():
            forward(PARTNER, RELAY, h, target).wait_recv()

        @pl.when(has_relay & ~same)
        def _():
            forward(RELAY, EXTRA, h, sibling).start()

    def compute(h):
        forward(OWN, SIB, h, sibling).wait_recv()

        @pl.when(has_relay | ~same)
        def _():
            forward(PARTNER, EXTRA, h, sibling).wait_recv()

        query = q_ref[:, columns(h)]
        grad = do_ref[:, columns(h)]
        scores, probs = [], []
        top = None
        for slot in range(SLOTS):
            raw = lax.dot_general(
                kv[slot, h, 0:TOK, :], query, (((1,), (1,)), ((), ())),
                preferred_element_type=jnp.float32,
            )
            parts = [
                raw[b * BLOCK:(b + 1) * BLOCK] * scale2
                + bias_ref[slot * BLOCKS + b:slot * BLOCKS + b + 1, :]
                for b in range(BLOCKS)
            ]
            score = jnp.concatenate(parts, axis=0)
            scores.append(score)
            peak = jnp.max(score, axis=0, keepdims=True)
            top = peak if top is None else jnp.maximum(top, peak)
        total = jnp.zeros((1, TOK), jnp.float32)
        dot = jnp.zeros((1, TOK), jnp.float32)
        weights = []
        for slot in range(SLOTS):
            prob = lax.dot_general(
                kv[slot, h, TOK:2 * TOK, :], grad, (((1,), (1,)), ((), ())),
                preferred_element_type=jnp.float32,
            )
            weight = jnp.exp2(scores[slot] - top)
            total = total + jnp.sum(weight, axis=0, keepdims=True)
            dot = dot + jnp.sum(weight * prob, axis=0, keepdims=True)
            weights.append(weight)
            probs.append(prob)
        inverse = 1.0 / total
        delta = dot * inverse
        query_grad = jnp.zeros((TOK, HDIM), jnp.float32)
        for slot in range(SLOTS):
            weight = weights[slot] * inverse
            low = weight.astype(jnp.bfloat16)
            grad_score = (weight * (probs[slot] - delta)).astype(jnp.bfloat16)
            value_part = jnp.dot(low, grad, preferred_element_type=jnp.float32)
            key_part = jnp.dot(grad_score, query, preferred_element_type=jnp.float32) * scale
            query_grad = query_grad + lax.dot_general(
                grad_score, kv[slot, h, 0:TOK, :], (((0,), (0,)), ((), ())),
                preferred_element_type=jnp.float32,
            )
            if slot in (SIB, EXTRA):
                back_out[slot - 1, h, 0:TOK, :] = key_part.astype(jnp.bfloat16)
                back_out[slot - 1, h, TOK:2 * TOK, :] = value_part.astype(jnp.bfloat16)
            else:
                acc = {OWN: own_acc, PARTNER: partner_acc, RELAY: relay_acc}[slot]
                acc[h, 0:TOK, :] = key_part
                acc[h, TOK:2 * TOK, :] = value_part
        dq_ref[:, columns(h)] = (query_grad * scale).astype(jnp.bfloat16)

        backward(SIB, h, sibling).start()

        @pl.when(has_relay | ~same)
        def _():
            backward(EXTRA, h, sibling).start()

    def return_relay(h):
        @pl.when(same)
        def _():
            backward(EXTRA, h, sibling).wait_recv()
            partner_acc[h] = partner_acc[h] + back_in[EXTRA - 1, h].astype(jnp.float32)

        @pl.when(has_relay & ~same)
        def _():
            backward(EXTRA, h, sibling).wait_recv()
            relay_acc[h] = relay_acc[h] + back_in[EXTRA - 1, h].astype(jnp.float32)

        @pl.when(has_relay)
        def _():
            back_out[RELAY - 1, h] = relay_acc[h].astype(jnp.bfloat16)
            backward(RELAY, h, source).start()

    def return_partner(h):
        @pl.when(has_target)
        def _():
            backward(RELAY, h, source).wait_recv()
            partner_acc[h] = partner_acc[h] + back_in[RELAY - 1, h].astype(jnp.float32)

        back_out[PARTNER - 1, h] = partner_acc[h].astype(jnp.bfloat16)
        backward(PARTNER, h, partner).start()

    def finish(h):
        backward(SIB, h, sibling).wait_recv()
        backward(PARTNER, h, partner).wait_recv()
        done = (
            own_acc[h]
            + back_in[SIB - 1, h].astype(jnp.float32)
            + back_in[PARTNER - 1, h].astype(jnp.float32)
        ).astype(jnp.bfloat16)
        dk_ref[:, columns(h)] = done[0:TOK]
        dv_ref[:, columns(h)] = done[TOK:2 * TOK]

    stages = (pass_partner, pass_relay, compute, return_relay, return_partner, finish)

    def step(at, carry):
        if AHEAD < heads:
            @pl.when(at + AHEAD < heads)
            def _():
                send_own(at + AHEAD)

        for lag, stage in enumerate(stages):
            @pl.when((at >= lag) & (at < heads + lag))
            def _(stage=stage, lag=lag):
                stage(at - lag)

        return carry

    lax.fori_loop(0, heads + len(stages) - 1, step, 0)

    def drain(h, carry):
        forward(OWN, PARTNER, h, partner).wait_send()
        forward(OWN, SIB, h, sibling).wait_send()
        backward(SIB, h, sibling).wait_send()
        backward(PARTNER, h, partner).wait_send()

        @pl.when(has_target)
        def _():
            forward(PARTNER, RELAY, h, target).wait_send()

        @pl.when(has_relay)
        def _():
            backward(RELAY, h, source).wait_send()

        @pl.when(same | has_relay)
        def _():
            forward(PARTNER, EXTRA, h, sibling).wait_send()

        @pl.when(~same | has_relay)
        def _():
            backward(EXTRA, h, sibling).wait_send()

        return carry

    lax.fori_loop(0, heads, drain, 0)


def local(tm_count, queries, keys, values, grad_out, block_list):
    heads = queries.shape[1] // HDIM
    bias = slot_bias(block_list, tm_count)
    out = jax.ShapeDtypeStruct(queries.shape, jnp.bfloat16)
    vmem = pl.BlockSpec(memory_space=pltpu.VMEM)
    pair = (heads, 2 * TOK, HDIM)
    return pl.pallas_call(
        functools.partial(kernel, tm_count, heads),
        out_shape=(out, out, out),
        in_specs=[vmem] * 5,
        out_specs=(vmem, vmem, vmem),
        scratch_shapes=[
            pltpu.VMEM((SLOTS,) + pair, jnp.bfloat16),
            pltpu.VMEM((SLOTS - 1,) + pair, jnp.bfloat16),
            pltpu.VMEM((SLOTS - 1,) + pair, jnp.bfloat16),
            pltpu.VMEM(pair, jnp.float32),
            pltpu.VMEM(pair, jnp.float32),
            pltpu.VMEM(pair, jnp.float32),
            pltpu.SemaphoreType.DMA((SLOTS - 1, heads)),
            pltpu.SemaphoreType.DMA((SLOTS - 1, heads)),
            pltpu.SemaphoreType.DMA((SLOTS - 1, heads)),
            pltpu.SemaphoreType.DMA((SLOTS - 1, heads)),
        ],
        compiler_params=pltpu.CompilerParams(
            collective_id=0, has_side_effects=True, vmem_limit_bytes=56 * 2**20
        ),
    )(queries, keys, values, grad_out, bias)


def solution(mesh):
    placed = P(("group", "tm"), None)
    return jax.shard_map(
        functools.partial(local, mesh.shape["tm"]),
        mesh=mesh,
        in_specs=(placed,) * 5,
        out_specs=(placed,) * 3,
        check_vma=False,
    )
```

```python
import functools
import math

import jax
import jax.numpy as jnp
from jax import lax
from jax.experimental import pallas as pl
from jax.experimental.pallas import tpu as pltpu
from jax.sharding import PartitionSpec as P

HDIM = 128
BLOCK = 64
REACH = 2
FRAMES = 2
BANDS = 2
SLOTS = 2 * REACH + 1
BLOCKS = FRAMES * BANDS
TOK = BLOCKS * BLOCK
MESH = pl.DeviceIdType.MESH
AHEAD = 12

OWN, SIB, PARTNER, EXTRA, RELAY = range(5)


def place(tm_count):
    here = lax.axis_index("tm")
    core = lax.rem(here, 2)
    half = lax.rem(here // 2, 2)
    column = here // 4
    columns = tm_count // 4
    down, up = column > 0, column < columns - 1
    even = half == 0
    has_relay = (even & down) | (~even & up)
    has_target = (even & up) | (~even & down)
    return here, core, half, down, up, has_relay, has_target


def slot_bias(block_list, tm_count):
    here, core, half, _, _, _, _ = place(tm_count)
    shape = (SLOTS * BLOCKS, BLOCKS, FRAMES * SLOTS * 3)
    key_block = lax.broadcasted_iota(jnp.int32, shape, 0)
    query_block = lax.broadcasted_iota(jnp.int32, shape, 1)
    slot = key_block // BLOCKS
    offset = jnp.where(
        slot == OWN, REACH,
        jnp.where(
            slot == SIB, 3 - 2 * core,
            jnp.where(
                slot == PARTNER, 4 - 4 * half,
                jnp.where(slot == EXTRA, 1 + 2 * core, 4 * half),
            ),
        ),
    )
    frame = key_block // BANDS % FRAMES
    band = key_block % BANDS
    cand = (offset * FRAMES + frame) * 3 + band - query_block % BANDS + 1
    group = here + offset - REACH
    exists = (group >= 0) & (group < tm_count)
    hit = exists & (lax.broadcasted_iota(jnp.int32, shape, 2) == cand)
    mine = (slot == OWN) & (key_block % BLOCKS == query_block)
    hits = (hit & (block_list > 0)[None]) | mine
    listed = jnp.max(hits.astype(jnp.float32), axis=2, keepdims=True)
    listed = jnp.broadcast_to(listed, (SLOTS * BLOCKS, BLOCKS, BLOCK))
    return jnp.where(listed > 0.5, 0.0, -jnp.inf).reshape(SLOTS * BLOCKS, TOK)


def kernel(
    tm_count, heads,
    q_ref, k_ref, v_ref, do_ref, bias_ref,
    dq_ref, dk_ref, dv_ref,
    kv, back_out, back_in, own_acc, partner_acc, relay_acc,
    fwd_send, fwd_recv, back_send, back_recv,
):
    here, core, half, down, up, has_relay, has_target = place(tm_count)
    sibling = here + 1 - 2 * core
    partner = here + 2 - 4 * half
    target = here + 4 - 8 * half
    source = here - 4 + 8 * half
    same = half == core
    scale = HDIM ** -0.5
    scale2 = scale * math.log2(math.e)

    barrier = pltpu.get_barrier_semaphore()

    def greet(device):
        pl.semaphore_signal(barrier, inc=1, device_id={"tm": device}, device_id_type=MESH)

    greet(sibling)
    greet(partner)

    @pl.when(down)
    def _():
        greet(here - 4)

    @pl.when(up)
    def _():
        greet(here + 4)

    def columns(h):
        return pl.ds(pl.multiple_of(h * HDIM, HDIM), HDIM)

    def pack(h, carry):
        kv[OWN, h, 0:TOK, :] = k_ref[:, columns(h)]
        kv[OWN, h, TOK:2 * TOK, :] = v_ref[:, columns(h)]
        return carry

    lax.fori_loop(0, heads, pack, 0)

    @pl.when(~has_relay)
    def _():
        def clear(h, carry):
            kv[RELAY, h] = jnp.zeros((2 * TOK, HDIM), jnp.bfloat16)
            return carry

        lax.fori_loop(0, heads, clear, 0)

    @pl.when(same & ~has_relay)
    def _():
        def clear(h, carry):
            kv[EXTRA, h] = jnp.zeros((2 * TOK, HDIM), jnp.bfloat16)
            return carry

        lax.fori_loop(0, heads, clear, 0)

    pl.semaphore_wait(barrier, 2 + down.astype(jnp.int32) + up.astype(jnp.int32))

    def forward(slot_from, slot_to, h, device):
        return pltpu.make_async_remote_copy(
            src_ref=kv.at[slot_from, h],
            dst_ref=kv.at[slot_to, h],
            send_sem=fwd_send.at[slot_to - 1, h],
            recv_sem=fwd_recv.at[slot_to - 1, h],
            device_id={"tm": device},
            device_id_type=MESH,
        )

    def backward(slot, h, device):
        return pltpu.make_async_remote_copy(
            src_ref=back_out.at[slot - 1, h],
            dst_ref=back_in.at[slot - 1, h],
            send_sem=back_send.at[slot - 1, h],
            recv_sem=back_recv.at[slot - 1, h],
            device_id={"tm": device},
            device_id_type=MESH,
        )

    def send_own(h):
        forward(OWN, PARTNER, h, partner).start()
        forward(OWN, SIB, h, sibling).start()

    def first(h, carry):
        send_own(h)
        return carry

    lax.fori_loop(0, min(AHEAD, heads), first, 0)

    def pass_partner(h):
        forward(OWN, PARTNER, h, partner).wait_recv()

        @pl.when(has_target)
        def _():
            forward(PARTNER, RELAY, h, target).start()

        @pl.when(same)
        def _():
            forward(PARTNER, EXTRA, h, sibling).start()

    def pass_relay(h):
        @pl.when(has_relay)
        def _():
            forward(PARTNER, RELAY, h, target).wait_recv()

        @pl.when(has_relay & ~same)
        def _():
            forward(RELAY, EXTRA, h, sibling).start()

    def compute(h):
        forward(OWN, SIB, h, sibling).wait_recv()

        @pl.when(has_relay | ~same)
        def _():
            forward(PARTNER, EXTRA, h, sibling).wait_recv()

        query = q_ref[:, columns(h)]
        grad = do_ref[:, columns(h)]
        scores, probs = [], []
        top = None
        for slot in range(SLOTS):
            raw = lax.dot_general(
                kv[slot, h, 0:TOK, :], query, (((1,), (1,)), ((), ())),
                preferred_element_type=jnp.float32,
            )
            parts = [
                raw[b * BLOCK:(b + 1) * BLOCK] * scale2
                + bias_ref[slot * BLOCKS + b:slot * BLOCKS + b + 1, :]
                for b in range(BLOCKS)
            ]
            score = jnp.concatenate(parts, axis=0)
            scores.append(score)
            peak = jnp.max(score, axis=0, keepdims=True)
            top = peak if top is None else jnp.maximum(top, peak)
        total = jnp.zeros((1, TOK), jnp.float32)
        dot = jnp.zeros((1, TOK), jnp.float32)
        weights = []
        for slot in range(SLOTS):
            prob = lax.dot_general(
                kv[slot, h, TOK:2 * TOK, :], grad, (((1,), (1,)), ((), ())),
                preferred_element_type=jnp.float32,
            )
            weight = jnp.exp2(scores[slot] - top)
            total = total + jnp.sum(weight, axis=0, keepdims=True)
            dot = dot + jnp.sum(weight * prob, axis=0, keepdims=True)
            weights.append(weight)
            probs.append(prob)
        inverse = 1.0 / total
        delta = dot * inverse
        query_grad = jnp.zeros((TOK, HDIM), jnp.float32)
        for slot in range(SLOTS):
            weight = weights[slot] * inverse
            low = weight.astype(jnp.bfloat16)
            grad_score = (weight * (probs[slot] - delta)).astype(jnp.bfloat16)
            value_part = jnp.dot(low, grad, preferred_element_type=jnp.float32)
            key_part = jnp.dot(grad_score, query, preferred_element_type=jnp.float32) * scale
            query_grad = query_grad + lax.dot_general(
                grad_score, kv[slot, h, 0:TOK, :], (((0,), (0,)), ((), ())),
                preferred_element_type=jnp.float32,
            )
            if slot in (SIB, EXTRA):
                back_out[slot - 1, h, 0:TOK, :] = key_part.astype(jnp.bfloat16)
                back_out[slot - 1, h, TOK:2 * TOK, :] = value_part.astype(jnp.bfloat16)
            else:
                acc = {OWN: own_acc, PARTNER: partner_acc, RELAY: relay_acc}[slot]
                acc[h, 0:TOK, :] = key_part
                acc[h, TOK:2 * TOK, :] = value_part
        dq_ref[:, columns(h)] = (query_grad * scale).astype(jnp.bfloat16)

        backward(SIB, h, sibling).start()

        @pl.when(has_relay | ~same)
        def _():
            backward(EXTRA, h, sibling).start()

    def return_relay(h):
        @pl.when(same)
        def _():
            backward(EXTRA, h, sibling).wait_recv()
            partner_acc[h] = partner_acc[h] + back_in[EXTRA - 1, h].astype(jnp.float32)

        @pl.when(has_relay & ~same)
        def _():
            backward(EXTRA, h, sibling).wait_recv()
            relay_acc[h] = relay_acc[h] + back_in[EXTRA - 1, h].astype(jnp.float32)

        @pl.when(has_relay)
        def _():
            back_out[RELAY - 1, h] = relay_acc[h].astype(jnp.bfloat16)
            backward(RELAY, h, source).start()

    def return_partner(h):
        @pl.when(has_target)
        def _():
            backward(RELAY, h, source).wait_recv()
            partner_acc[h] = partner_acc[h] + back_in[RELAY - 1, h].astype(jnp.float32)

        back_out[PARTNER - 1, h] = partner_acc[h].astype(jnp.bfloat16)
        backward(PARTNER, h, partner).start()

    def finish(h):
        backward(SIB, h, sibling).wait_recv()
        backward(PARTNER, h, partner).wait_recv()
        done = (
            own_acc[h]
            + back_in[SIB - 1, h].astype(jnp.float32)
            + back_in[PARTNER - 1, h].astype(jnp.float32)
        ).astype(jnp.bfloat16)
        dk_ref[:, columns(h)] = done[0:TOK]
        dv_ref[:, columns(h)] = done[TOK:2 * TOK]

    stages = (
        (0, pass_partner), (1, pass_relay), (6, return_partner), (4, return_relay), (2, compute),
    )

    def step(at, carry):
        if AHEAD < heads:
            @pl.when(at + AHEAD < heads)
            def _():
                send_own(at + AHEAD)

        for lag, stage in stages:
            @pl.when((at >= lag) & (at < heads + lag))
            def _(stage=stage, lag=lag):
                stage(at - lag)

        return carry

    lax.fori_loop(0, heads + max(lag for lag, _ in stages), step, 0)

    def last(h, carry):
        finish(h)
        return carry

    lax.fori_loop(0, heads, last, 0)

    def drain(h, carry):
        forward(OWN, PARTNER, h, partner).wait_send()
        forward(OWN, SIB, h, sibling).wait_send()
        backward(SIB, h, sibling).wait_send()
        backward(PARTNER, h, partner).wait_send()

        @pl.when(has_target)
        def _():
            forward(PARTNER, RELAY, h, target).wait_send()

        @pl.when(has_relay)
        def _():
            backward(RELAY, h, source).wait_send()

        @pl.when(same | has_relay)
        def _():
            forward(PARTNER, EXTRA, h, sibling).wait_send()

        @pl.when(~same | has_relay)
        def _():
            backward(EXTRA, h, sibling).wait_send()

        return carry

    lax.fori_loop(0, heads, drain, 0)


def local(tm_count, queries, keys, values, grad_out, block_list):
    heads = queries.shape[1] // HDIM
    bias = slot_bias(block_list, tm_count)
    out = jax.ShapeDtypeStruct(queries.shape, jnp.bfloat16)
    vmem = pl.BlockSpec(memory_space=pltpu.VMEM)
    pair = (heads, 2 * TOK, HDIM)
    return pl.pallas_call(
        functools.partial(kernel, tm_count, heads),
        out_shape=(out, out, out),
        in_specs=[vmem] * 5,
        out_specs=(vmem, vmem, vmem),
        scratch_shapes=[
            pltpu.VMEM((SLOTS,) + pair, jnp.bfloat16),
            pltpu.VMEM((SLOTS - 1,) + pair, jnp.bfloat16),
            pltpu.VMEM((SLOTS - 1,) + pair, jnp.bfloat16),
            pltpu.VMEM(pair, jnp.float32),
            pltpu.VMEM(pair, jnp.float32),
            pltpu.VMEM(pair, jnp.float32),
            pltpu.SemaphoreType.DMA((SLOTS - 1, heads)),
            pltpu.SemaphoreType.DMA((SLOTS - 1, heads)),
            pltpu.SemaphoreType.DMA((SLOTS - 1, heads)),
            pltpu.SemaphoreType.DMA((SLOTS - 1, heads)),
        ],
        compiler_params=pltpu.CompilerParams(
            collective_id=0, has_side_effects=True, vmem_limit_bytes=56 * 2**20
        ),
    )(queries, keys, values, grad_out, bias)


def solution(mesh):
    placed = P(("group", "tm"), None)
    return jax.shard_map(
        functools.partial(local, mesh.shape["tm"]),
        mesh=mesh,
        in_specs=(placed,) * 5,
        out_specs=(placed,) * 3,
        check_vma=False,
    )
```

```python
import functools
import math

import jax
import jax.numpy as jnp
from jax import lax
from jax.experimental import pallas as pl
from jax.experimental.pallas import tpu as pltpu
from jax.sharding import PartitionSpec as P

HDIM = 128
BLOCK = 64
REACH = 2
FRAMES = 2
BANDS = 2
SLOTS = 2 * REACH + 1
BLOCKS = FRAMES * BANDS
TOK = BLOCKS * BLOCK
MESH = pl.DeviceIdType.MESH
AHEAD = 4

OWN, SIB, PARTNER, EXTRA, RELAY = range(5)


def place(tm_count):
    here = lax.axis_index("tm")
    core = lax.rem(here, 2)
    half = lax.rem(here // 2, 2)
    column = here // 4
    columns = tm_count // 4
    down, up = column > 0, column < columns - 1
    even = half == 0
    has_relay = (even & down) | (~even & up)
    has_target = (even & up) | (~even & down)
    return here, core, half, down, up, has_relay, has_target


def slot_bias(block_list, tm_count):
    here, core, half, _, _, _, _ = place(tm_count)
    shape = (SLOTS * BLOCKS, BLOCKS, FRAMES * SLOTS * 3)
    key_block = lax.broadcasted_iota(jnp.int32, shape, 0)
    query_block = lax.broadcasted_iota(jnp.int32, shape, 1)
    slot = key_block // BLOCKS
    offset = jnp.where(
        slot == OWN, REACH,
        jnp.where(
            slot == SIB, 3 - 2 * core,
            jnp.where(
                slot == PARTNER, 4 - 4 * half,
                jnp.where(slot == EXTRA, 1 + 2 * core, 4 * half),
            ),
        ),
    )
    frame = key_block // BANDS % FRAMES
    band = key_block % BANDS
    cand = (offset * FRAMES + frame) * 3 + band - query_block % BANDS + 1
    group = here + offset - REACH
    exists = (group >= 0) & (group < tm_count)
    hit = exists & (lax.broadcasted_iota(jnp.int32, shape, 2) == cand)
    mine = (slot == OWN) & (key_block % BLOCKS == query_block)
    hits = (hit & (block_list > 0)[None]) | mine
    listed = jnp.max(hits.astype(jnp.float32), axis=2, keepdims=True)
    listed = jnp.broadcast_to(listed, (SLOTS * BLOCKS, BLOCKS, BLOCK))
    return jnp.where(listed > 0.5, 0.0, -jnp.inf).reshape(SLOTS * BLOCKS, TOK)


def kernel(
    tm_count, heads,
    q_ref, k_ref, v_ref, do_ref, bias_ref,
    dq_ref, dk_ref, dv_ref,
    q_buf, do_buf, kv, back_out, back_in, own_acc, partner_acc, relay_acc,
    row_sem, load_sem, fwd_send, fwd_recv, back_send, back_recv,
):
    here, core, half, down, up, has_relay, has_target = place(tm_count)
    sibling = here + 1 - 2 * core
    partner = here + 2 - 4 * half
    target = here + 4 - 8 * half
    source = here - 4 + 8 * half
    same = half == core
    scale = HDIM ** -0.5
    scale2 = scale * math.log2(math.e)

    barrier = pltpu.get_barrier_semaphore()

    def greet(device):
        pl.semaphore_signal(barrier, inc=1, device_id={"tm": device}, device_id_type=MESH)

    greet(sibling)
    greet(partner)

    @pl.when(down)
    def _():
        greet(here - 4)

    @pl.when(up)
    def _():
        greet(here + 4)

    def columns(h):
        return pl.ds(pl.multiple_of(h * HDIM, HDIM), HDIM)

    def load(which, ref, h):
        return pltpu.make_async_copy(
            ref.at[:, columns(h)],
            kv.at[OWN, h, pl.ds(which * TOK, TOK)],
            load_sem.at[which, h],
        )

    def begin(h, carry):
        load(0, k_ref, h).start()
        load(1, v_ref, h).start()
        return carry

    lax.fori_loop(0, heads, begin, 0)
    rows = (
        pltpu.make_async_copy(q_ref, q_buf, row_sem.at[0]),
        pltpu.make_async_copy(do_ref, do_buf, row_sem.at[1]),
    )
    for row in rows:
        row.start()

    @pl.when(~has_relay)
    def _():
        def clear(h, carry):
            kv[RELAY, h] = jnp.zeros((2 * TOK, HDIM), jnp.bfloat16)
            return carry

        lax.fori_loop(0, heads, clear, 0)

    @pl.when(same & ~has_relay)
    def _():
        def clear(h, carry):
            kv[EXTRA, h] = jnp.zeros((2 * TOK, HDIM), jnp.bfloat16)
            return carry

        lax.fori_loop(0, heads, clear, 0)

    pl.semaphore_wait(barrier, 2 + down.astype(jnp.int32) + up.astype(jnp.int32))

    def forward(slot_from, slot_to, h, device):
        return pltpu.make_async_remote_copy(
            src_ref=kv.at[slot_from, h],
            dst_ref=kv.at[slot_to, h],
            send_sem=fwd_send.at[slot_to - 1, h],
            recv_sem=fwd_recv.at[slot_to - 1, h],
            device_id={"tm": device},
            device_id_type=MESH,
        )

    def backward(slot, h, device):
        return pltpu.make_async_remote_copy(
            src_ref=back_out.at[slot - 1, h],
            dst_ref=back_in.at[slot - 1, h],
            send_sem=back_send.at[slot - 1, h],
            recv_sem=back_recv.at[slot - 1, h],
            device_id={"tm": device},
            device_id_type=MESH,
        )

    def send_own(h):
        load(0, k_ref, h).wait()
        load(1, v_ref, h).wait()
        forward(OWN, PARTNER, h, partner).start()
        forward(OWN, SIB, h, sibling).start()

    def first(h, carry):
        send_own(h)
        return carry

    lax.fori_loop(0, min(AHEAD, heads), first, 0)

    for row in rows:
        row.wait()

    def pass_partner(h):
        forward(OWN, PARTNER, h, partner).wait_recv()

        @pl.when(has_target)
        def _():
            forward(PARTNER, RELAY, h, target).start()

        @pl.when(same)
        def _():
            forward(PARTNER, EXTRA, h, sibling).start()

    def pass_relay(h):
        @pl.when(has_relay)
        def _():
            forward(PARTNER, RELAY, h, target).wait_recv()

        @pl.when(has_relay & ~same)
        def _():
            forward(RELAY, EXTRA, h, sibling).start()

    def compute(h):
        forward(OWN, SIB, h, sibling).wait_recv()

        @pl.when(has_relay | ~same)
        def _():
            forward(PARTNER, EXTRA, h, sibling).wait_recv()

        query = q_buf[:, columns(h)]
        grad = do_buf[:, columns(h)]
        scores, probs = [], []
        top = None
        for slot in range(SLOTS):
            raw = lax.dot_general(
                kv[slot, h, 0:TOK, :], query, (((1,), (1,)), ((), ())),
                preferred_element_type=jnp.float32,
            )
            parts = [
                raw[b * BLOCK:(b + 1) * BLOCK] * scale2
                + bias_ref[slot * BLOCKS + b:slot * BLOCKS + b + 1, :]
                for b in range(BLOCKS)
            ]
            score = jnp.concatenate(parts, axis=0)
            scores.append(score)
            peak = jnp.max(score, axis=0, keepdims=True)
            top = peak if top is None else jnp.maximum(top, peak)
        total = jnp.zeros((1, TOK), jnp.float32)
        dot = jnp.zeros((1, TOK), jnp.float32)
        weights = []
        for slot in range(SLOTS):
            prob = lax.dot_general(
                kv[slot, h, TOK:2 * TOK, :], grad, (((1,), (1,)), ((), ())),
                preferred_element_type=jnp.float32,
            )
            weight = jnp.exp2(scores[slot] - top)
            total = total + jnp.sum(weight, axis=0, keepdims=True)
            dot = dot + jnp.sum(weight * prob, axis=0, keepdims=True)
            weights.append(weight)
            probs.append(prob)
        inverse = 1.0 / total
        delta = dot * inverse
        query_grad = jnp.zeros((TOK, HDIM), jnp.float32)
        for slot in range(SLOTS):
            weight = weights[slot] * inverse
            low = weight.astype(jnp.bfloat16)
            grad_score = (weight * (probs[slot] - delta)).astype(jnp.bfloat16)
            value_part = jnp.dot(low, grad, preferred_element_type=jnp.float32)
            key_part = jnp.dot(grad_score, query, preferred_element_type=jnp.float32) * scale
            query_grad = query_grad + lax.dot_general(
                grad_score, kv[slot, h, 0:TOK, :], (((0,), (0,)), ((), ())),
                preferred_element_type=jnp.float32,
            )
            if slot in (SIB, EXTRA):
                back_out[slot - 1, h, 0:TOK, :] = key_part.astype(jnp.bfloat16)
                back_out[slot - 1, h, TOK:2 * TOK, :] = value_part.astype(jnp.bfloat16)
            else:
                acc = {OWN: own_acc, PARTNER: partner_acc, RELAY: relay_acc}[slot]
                acc[h, 0:TOK, :] = key_part
                acc[h, TOK:2 * TOK, :] = value_part
        dq_ref[:, columns(h)] = (query_grad * scale).astype(jnp.bfloat16)

        backward(SIB, h, sibling).start()

        @pl.when(has_relay | ~same)
        def _():
            backward(EXTRA, h, sibling).start()

    def return_relay(h):
        @pl.when(same)
        def _():
            backward(EXTRA, h, sibling).wait_recv()
            partner_acc[h] = partner_acc[h] + back_in[EXTRA - 1, h].astype(jnp.float32)

        @pl.when(has_relay & ~same)
        def _():
            backward(EXTRA, h, sibling).wait_recv()
            relay_acc[h] = relay_acc[h] + back_in[EXTRA - 1, h].astype(jnp.float32)

        @pl.when(has_relay)
        def _():
            back_out[RELAY - 1, h] = relay_acc[h].astype(jnp.bfloat16)
            backward(RELAY, h, source).start()

    def return_partner(h):
        @pl.when(has_target)
        def _():
            backward(RELAY, h, source).wait_recv()
            partner_acc[h] = partner_acc[h] + back_in[RELAY - 1, h].astype(jnp.float32)

        back_out[PARTNER - 1, h] = partner_acc[h].astype(jnp.bfloat16)
        backward(PARTNER, h, partner).start()

    def finish(h):
        backward(SIB, h, sibling).wait_recv()
        backward(PARTNER, h, partner).wait_recv()
        done = (
            own_acc[h]
            + back_in[SIB - 1, h].astype(jnp.float32)
            + back_in[PARTNER - 1, h].astype(jnp.float32)
        ).astype(jnp.bfloat16)
        dk_ref[:, columns(h)] = done[0:TOK]
        dv_ref[:, columns(h)] = done[TOK:2 * TOK]

    stages = (
        (0, pass_partner), (1, pass_relay), (6, return_partner), (4, return_relay), (2, compute),
    )

    def step(at, carry):
        if AHEAD < heads:
            @pl.when(at + AHEAD < heads)
            def _():
                send_own(at + AHEAD)

        for lag, stage in stages:
            @pl.when((at >= lag) & (at < heads + lag))
            def _(stage=stage, lag=lag):
                stage(at - lag)

        return carry

    lax.fori_loop(0, heads + max(lag for lag, _ in stages), step, 0)

    def last(h, carry):
        finish(h)
        return carry

    lax.fori_loop(0, heads, last, 0)

    def drain(h, carry):
        forward(OWN, PARTNER, h, partner).wait_send()
        forward(OWN, SIB, h, sibling).wait_send()
        backward(SIB, h, sibling).wait_send()
        backward(PARTNER, h, partner).wait_send()

        @pl.when(has_target)
        def _():
            forward(PARTNER, RELAY, h, target).wait_send()

        @pl.when(has_relay)
        def _():
            backward(RELAY, h, source).wait_send()

        @pl.when(same | has_relay)
        def _():
            forward(PARTNER, EXTRA, h, sibling).wait_send()

        @pl.when(~same | has_relay)
        def _():
            backward(EXTRA, h, sibling).wait_send()

        return carry

    lax.fori_loop(0, heads, drain, 0)


def local(tm_count, queries, keys, values, grad_out, block_list):
    heads = queries.shape[1] // HDIM
    bias = slot_bias(block_list, tm_count)
    out = jax.ShapeDtypeStruct(queries.shape, jnp.bfloat16)
    vmem = pl.BlockSpec(memory_space=pltpu.VMEM)
    pair = (heads, 2 * TOK, HDIM)
    return pl.pallas_call(
        functools.partial(kernel, tm_count, heads),
        out_shape=(out, out, out),
        in_specs=[pl.BlockSpec(memory_space=pl.ANY)] * 4 + [vmem],
        out_specs=(vmem, vmem, vmem),
        scratch_shapes=[
            pltpu.VMEM(queries.shape, jnp.bfloat16),
            pltpu.VMEM(queries.shape, jnp.bfloat16),
            pltpu.VMEM((SLOTS,) + pair, jnp.bfloat16),
            pltpu.VMEM((SLOTS - 1,) + pair, jnp.bfloat16),
            pltpu.VMEM((SLOTS - 1,) + pair, jnp.bfloat16),
            pltpu.VMEM(pair, jnp.float32),
            pltpu.VMEM(pair, jnp.float32),
            pltpu.VMEM(pair, jnp.float32),
            pltpu.SemaphoreType.DMA((2,)),
            pltpu.SemaphoreType.DMA((2, heads)),
            pltpu.SemaphoreType.DMA((SLOTS - 1, heads)),
            pltpu.SemaphoreType.DMA((SLOTS - 1, heads)),
            pltpu.SemaphoreType.DMA((SLOTS - 1, heads)),
            pltpu.SemaphoreType.DMA((SLOTS - 1, heads)),
        ],
        compiler_params=pltpu.CompilerParams(
            collective_id=0, has_side_effects=True, vmem_limit_bytes=56 * 2**20
        ),
    )(queries, keys, values, grad_out, bias)


def solution(mesh):
    placed = P(("group", "tm"), None)
    return jax.shard_map(
        functools.partial(local, mesh.shape["tm"]),
        mesh=mesh,
        in_specs=(placed,) * 5,
        out_specs=(placed,) * 3,
        check_vma=False,
    )
```

```python
import functools
import math

import jax
import jax.numpy as jnp
from jax import lax
from jax.experimental import pallas as pl
from jax.experimental.pallas import tpu as pltpu
from jax.sharding import PartitionSpec as P

HDIM = 128
BLOCK = 64
REACH = 2
FRAMES = 2
BANDS = 2
SLOTS = 2 * REACH + 1
BLOCKS = FRAMES * BANDS
TOK = BLOCKS * BLOCK
MESH = pl.DeviceIdType.MESH
AHEAD = 4

OWN, SIB, PARTNER, EXTRA, RELAY = range(5)


def place(tm_count):
    here = lax.axis_index("tm")
    core = lax.rem(here, 2)
    half = lax.rem(here // 2, 2)
    column = here // 4
    columns = tm_count // 4
    down, up = column > 0, column < columns - 1
    even = half == 0
    has_relay = (even & down) | (~even & up)
    has_target = (even & up) | (~even & down)
    return here, core, half, down, up, has_relay, has_target


def kernel(
    tm_count, heads,
    q_ref, k_ref, v_ref, do_ref, list_ref,
    dq_ref, dk_ref, dv_ref,
    bias_ref, q_buf, do_buf, dq_buf, out_buf, kv, back_out, back_in, own_acc, partner_acc, relay_acc,
    row_sem, load_sem, store_sem, fwd_send, fwd_recv, back_send, back_recv,
):
    here, core, half, down, up, has_relay, has_target = place(tm_count)
    sibling = here + 1 - 2 * core
    partner = here + 2 - 4 * half
    target = here + 4 - 8 * half
    source = here - 4 + 8 * half
    same = half == core
    scale = HDIM ** -0.5
    scale2 = scale * math.log2(math.e)

    barrier = pltpu.get_barrier_semaphore()

    def greet(device):
        pl.semaphore_signal(barrier, inc=1, device_id={"tm": device}, device_id_type=MESH)

    greet(sibling)
    greet(partner)

    @pl.when(down)
    def _():
        greet(here - 4)

    @pl.when(up)
    def _():
        greet(here + 4)

    def columns(h):
        return pl.ds(pl.multiple_of(h * HDIM, HDIM), HDIM)

    def load(which, ref, h):
        return pltpu.make_async_copy(
            ref.at[:, columns(h)],
            kv.at[OWN, h, pl.ds(which * TOK, TOK)],
            load_sem.at[which, h],
        )

    def begin(h, carry):
        load(0, k_ref, h).start()
        load(1, v_ref, h).start()
        return carry

    lax.fori_loop(0, heads, begin, 0)
    rows = (
        pltpu.make_async_copy(q_ref, q_buf, row_sem.at[0]),
        pltpu.make_async_copy(do_ref, do_buf, row_sem.at[1]),
    )
    for row in rows:
        row.start()

    offsets = (REACH, 3 - 2 * core, 4 - 4 * half, 1 + 2 * core, 4 * half)
    query_block = lax.broadcasted_iota(jnp.int32, (1, TOK), 1) // BLOCK
    for slot in range(SLOTS):
        group = here + offsets[slot] - REACH
        exists = ((group >= 0) & (group < tm_count)).astype(jnp.int32)
        for key_block in range(BLOCKS):
            frame, band = key_block // BANDS, key_block % BANDS
            row = jnp.zeros((1, TOK), jnp.int32)
            for at in range(BLOCKS):
                if slot == OWN and at == key_block:
                    listed = 1
                else:
                    cand = (offsets[slot] * FRAMES + frame) * 3 + band - at % BANDS + 1
                    listed = list_ref[at, cand] * exists
                row = jnp.where(query_block == at, listed, row)
            index = slot * BLOCKS + key_block
            bias_ref[index:index + 1, :] = jnp.where(row > 0, 0.0, -jnp.inf)

    @pl.when(~has_relay)
    def _():
        def clear(h, carry):
            kv[RELAY, h] = jnp.zeros((2 * TOK, HDIM), jnp.bfloat16)
            return carry

        lax.fori_loop(0, heads, clear, 0)

    @pl.when(same & ~has_relay)
    def _():
        def clear(h, carry):
            kv[EXTRA, h] = jnp.zeros((2 * TOK, HDIM), jnp.bfloat16)
            return carry

        lax.fori_loop(0, heads, clear, 0)

    pl.semaphore_wait(barrier, 2 + down.astype(jnp.int32) + up.astype(jnp.int32))

    def forward(slot_from, slot_to, h, device):
        return pltpu.make_async_remote_copy(
            src_ref=kv.at[slot_from, h],
            dst_ref=kv.at[slot_to, h],
            send_sem=fwd_send.at[slot_to - 1, h],
            recv_sem=fwd_recv.at[slot_to - 1, h],
            device_id={"tm": device},
            device_id_type=MESH,
        )

    def backward(slot, h, device):
        return pltpu.make_async_remote_copy(
            src_ref=back_out.at[slot - 1, h],
            dst_ref=back_in.at[slot - 1, h],
            send_sem=back_send.at[slot - 1, h],
            recv_sem=back_recv.at[slot - 1, h],
            device_id={"tm": device},
            device_id_type=MESH,
        )

    def store(which, h):
        src = dq_buf.at[h] if which == 0 else out_buf.at[h, pl.ds((which - 1) * TOK, TOK)]
        return pltpu.make_async_copy(
            src, (dq_ref, dk_ref, dv_ref)[which].at[:, columns(h)], store_sem.at[which, h]
        )

    def send_own(h):
        load(0, k_ref, h).wait()
        load(1, v_ref, h).wait()
        forward(OWN, PARTNER, h, partner).start()
        forward(OWN, SIB, h, sibling).start()

    def first(h, carry):
        send_own(h)
        return carry

    lax.fori_loop(0, min(AHEAD, heads), first, 0)

    for row in rows:
        row.wait()

    def pass_partner(h):
        forward(OWN, PARTNER, h, partner).wait_recv()

        @pl.when(has_target)
        def _():
            forward(PARTNER, RELAY, h, target).start()

        @pl.when(same)
        def _():
            forward(PARTNER, EXTRA, h, sibling).start()

    def pass_relay(h):
        @pl.when(has_relay)
        def _():
            forward(PARTNER, RELAY, h, target).wait_recv()

        @pl.when(has_relay & ~same)
        def _():
            forward(RELAY, EXTRA, h, sibling).start()

    def compute(h):
        forward(OWN, SIB, h, sibling).wait_recv()

        @pl.when(has_relay | ~same)
        def _():
            forward(PARTNER, EXTRA, h, sibling).wait_recv()

        query = q_buf[:, columns(h)]
        grad = do_buf[:, columns(h)]
        scores, probs = [], []
        top = None
        for slot in range(SLOTS):
            raw = lax.dot_general(
                kv[slot, h, 0:TOK, :], query, (((1,), (1,)), ((), ())),
                preferred_element_type=jnp.float32,
            )
            parts = [
                raw[b * BLOCK:(b + 1) * BLOCK] * scale2
                + bias_ref[slot * BLOCKS + b:slot * BLOCKS + b + 1, :]
                for b in range(BLOCKS)
            ]
            score = jnp.concatenate(parts, axis=0)
            scores.append(score)
            peak = jnp.max(score, axis=0, keepdims=True)
            top = peak if top is None else jnp.maximum(top, peak)
        total = jnp.zeros((1, TOK), jnp.float32)
        dot = jnp.zeros((1, TOK), jnp.float32)
        weights = []
        for slot in range(SLOTS):
            prob = lax.dot_general(
                kv[slot, h, TOK:2 * TOK, :], grad, (((1,), (1,)), ((), ())),
                preferred_element_type=jnp.float32,
            )
            weight = jnp.exp2(scores[slot] - top)
            total = total + jnp.sum(weight, axis=0, keepdims=True)
            dot = dot + jnp.sum(weight * prob, axis=0, keepdims=True)
            weights.append(weight)
            probs.append(prob)
        inverse = 1.0 / total
        delta = dot * inverse
        query_grad = jnp.zeros((TOK, HDIM), jnp.float32)
        for slot in range(SLOTS):
            weight = weights[slot] * inverse
            low = weight.astype(jnp.bfloat16)
            grad_score = (weight * (probs[slot] - delta)).astype(jnp.bfloat16)
            value_part = jnp.dot(low, grad, preferred_element_type=jnp.float32)
            key_part = jnp.dot(grad_score, query, preferred_element_type=jnp.float32) * scale
            query_grad = query_grad + lax.dot_general(
                grad_score, kv[slot, h, 0:TOK, :], (((0,), (0,)), ((), ())),
                preferred_element_type=jnp.float32,
            )
            if slot in (SIB, EXTRA):
                back_out[slot - 1, h, 0:TOK, :] = key_part.astype(jnp.bfloat16)
                back_out[slot - 1, h, TOK:2 * TOK, :] = value_part.astype(jnp.bfloat16)
            else:
                acc = {OWN: own_acc, PARTNER: partner_acc, RELAY: relay_acc}[slot]
                acc[h, 0:TOK, :] = key_part
                acc[h, TOK:2 * TOK, :] = value_part
        dq_buf[h] = (query_grad * scale).astype(jnp.bfloat16)
        store(0, h).start()

        backward(SIB, h, sibling).start()

        @pl.when(has_relay | ~same)
        def _():
            backward(EXTRA, h, sibling).start()

    def return_relay(h):
        @pl.when(same)
        def _():
            backward(EXTRA, h, sibling).wait_recv()
            partner_acc[h] = partner_acc[h] + back_in[EXTRA - 1, h].astype(jnp.float32)

        @pl.when(has_relay & ~same)
        def _():
            backward(EXTRA, h, sibling).wait_recv()
            relay_acc[h] = relay_acc[h] + back_in[EXTRA - 1, h].astype(jnp.float32)

        @pl.when(has_relay)
        def _():
            back_out[RELAY - 1, h] = relay_acc[h].astype(jnp.bfloat16)
            backward(RELAY, h, source).start()

    def return_partner(h):
        @pl.when(has_target)
        def _():
            backward(RELAY, h, source).wait_recv()
            partner_acc[h] = partner_acc[h] + back_in[RELAY - 1, h].astype(jnp.float32)

        back_out[PARTNER - 1, h] = partner_acc[h].astype(jnp.bfloat16)
        backward(PARTNER, h, partner).start()

    def finish(h):
        backward(SIB, h, sibling).wait_recv()
        backward(PARTNER, h, partner).wait_recv()
        done = (
            own_acc[h]
            + back_in[SIB - 1, h].astype(jnp.float32)
            + back_in[PARTNER - 1, h].astype(jnp.float32)
        ).astype(jnp.bfloat16)
        out_buf[h] = done
        store(1, h).start()
        store(2, h).start()

    stages = (
        (0, pass_partner), (1, pass_relay), (6, return_partner), (4, return_relay), (2, compute),
    )

    def step(at, carry):
        if AHEAD < heads:
            @pl.when(at + AHEAD < heads)
            def _():
                send_own(at + AHEAD)

        for lag, stage in stages:
            @pl.when((at >= lag) & (at < heads + lag))
            def _(stage=stage, lag=lag):
                stage(at - lag)

        return carry

    lax.fori_loop(0, heads + max(lag for lag, _ in stages), step, 0)

    def last(h, carry):
        finish(h)
        return carry

    lax.fori_loop(0, heads, last, 0)

    def drain(h, carry):
        for which in range(3):
            store(which, h).wait()
        forward(OWN, PARTNER, h, partner).wait_send()
        forward(OWN, SIB, h, sibling).wait_send()
        backward(SIB, h, sibling).wait_send()
        backward(PARTNER, h, partner).wait_send()

        @pl.when(has_target)
        def _():
            forward(PARTNER, RELAY, h, target).wait_send()

        @pl.when(has_relay)
        def _():
            backward(RELAY, h, source).wait_send()

        @pl.when(same | has_relay)
        def _():
            forward(PARTNER, EXTRA, h, sibling).wait_send()

        @pl.when(~same | has_relay)
        def _():
            backward(EXTRA, h, sibling).wait_send()

        return carry

    lax.fori_loop(0, heads, drain, 0)


def settle_kernel(*refs):
    sources, results, sems = refs[:3], refs[3:6], refs[6]
    copies = [
        pltpu.make_async_copy(
            src.at[pl.ds(part * BLOCK, BLOCK)], dst.at[pl.ds(part * BLOCK, BLOCK)], sems.at[i, part]
        )
        for i, (src, dst) in enumerate(zip(sources, results))
        for part in range(BLOCKS)
    ]
    for copy in copies:
        copy.start()
    for copy in copies:
        copy.wait()


def local(tm_count, queries, keys, values, grad_out, block_list):
    heads = queries.shape[1] // HDIM
    out = jax.ShapeDtypeStruct(queries.shape, jnp.bfloat16)
    hbm = pl.BlockSpec(memory_space=pl.ANY)
    pair = (heads, 2 * TOK, HDIM)
    grads = pl.pallas_call(
        functools.partial(kernel, tm_count, heads),
        out_shape=(out,) * 3,
        in_specs=[hbm] * 4 + [pl.BlockSpec(memory_space=pltpu.SMEM)],
        out_specs=(hbm,) * 3,
        scratch_shapes=[
            pltpu.VMEM((SLOTS * BLOCKS, TOK), jnp.float32),
            pltpu.VMEM(queries.shape, jnp.bfloat16),
            pltpu.VMEM(queries.shape, jnp.bfloat16),
            pltpu.VMEM((heads, TOK, HDIM), jnp.bfloat16),
            pltpu.VMEM(pair, jnp.bfloat16),
            pltpu.VMEM((SLOTS,) + pair, jnp.bfloat16),
            pltpu.VMEM((SLOTS - 1,) + pair, jnp.bfloat16),
            pltpu.VMEM((SLOTS - 1,) + pair, jnp.bfloat16),
            pltpu.VMEM(pair, jnp.float32),
            pltpu.VMEM(pair, jnp.float32),
            pltpu.VMEM(pair, jnp.float32),
            pltpu.SemaphoreType.DMA((2,)),
            pltpu.SemaphoreType.DMA((2, heads)),
            pltpu.SemaphoreType.DMA((3, heads)),
            pltpu.SemaphoreType.DMA((SLOTS - 1, heads)),
            pltpu.SemaphoreType.DMA((SLOTS - 1, heads)),
            pltpu.SemaphoreType.DMA((SLOTS - 1, heads)),
            pltpu.SemaphoreType.DMA((SLOTS - 1, heads)),
        ],
        compiler_params=pltpu.CompilerParams(
            collective_id=0, has_side_effects=True, vmem_limit_bytes=56 * 2**20
        ),
    )(queries, keys, values, grad_out, block_list)
    return pl.pallas_call(
        settle_kernel,
        out_shape=(out,) * 3,
        in_specs=[hbm] * 3,
        out_specs=(hbm,) * 3,
        scratch_shapes=[pltpu.SemaphoreType.DMA((3, BLOCKS))],
        compiler_params=pltpu.CompilerParams(vmem_limit_bytes=56 * 2**20),
    )(*grads)


def solution(mesh):
    placed = P(("group", "tm"), None)
    return jax.shard_map(
        functools.partial(local, mesh.shape["tm"]),
        mesh=mesh,
        in_specs=(placed,) * 5,
        out_specs=(placed,) * 3,
        check_vma=False,
    )
```

```python
import functools
import math

import jax
import jax.numpy as jnp
from jax import lax
from jax.experimental import pallas as pl
from jax.experimental.pallas import tpu as pltpu
from jax.sharding import PartitionSpec as P

HDIM = 128
BLOCK = 64
REACH = 2
FRAMES = 2
BANDS = 2
SLOTS = 2 * REACH + 1
BLOCKS = FRAMES * BANDS
TOK = BLOCKS * BLOCK
MESH = pl.DeviceIdType.MESH
AHEAD = 4

OWN, SIB, PARTNER, EXTRA, RELAY = range(5)


def place(tm_count):
    here = lax.axis_index("tm")
    core = lax.rem(here, 2)
    half = lax.rem(here // 2, 2)
    column = here // 4
    columns = tm_count // 4
    down, up = column > 0, column < columns - 1
    even = half == 0
    has_relay = (even & down) | (~even & up)
    has_target = (even & up) | (~even & down)
    return here, core, half, down, up, has_relay, has_target


def kernel(
    tm_count, heads,
    q_ref, k_ref, v_ref, do_ref, list_ref,
    dq_ref, dk_ref, dv_ref,
    bias_ref, q_buf, do_buf, dq_buf, out_buf, kv, back_out, back_in, own_acc, partner_acc, relay_acc,
    row_sem, load_sem, store_sem, fwd_send, fwd_recv, back_send, back_recv,
):
    here, core, half, down, up, has_relay, has_target = place(tm_count)
    sibling = here + 1 - 2 * core
    partner = here + 2 - 4 * half
    target = here + 4 - 8 * half
    source = here - 4 + 8 * half
    same = half == core
    scale = HDIM ** -0.5
    scale2 = scale * math.log2(math.e)

    barrier = pltpu.get_barrier_semaphore()

    def greet(device):
        pl.semaphore_signal(barrier, inc=1, device_id={"tm": device}, device_id_type=MESH)

    greet(sibling)
    greet(partner)

    @pl.when(down)
    def _():
        greet(here - 4)

    @pl.when(up)
    def _():
        greet(here + 4)

    def columns(h):
        return pl.ds(pl.multiple_of(h * HDIM, HDIM), HDIM)

    def load(which, ref, h):
        return pltpu.make_async_copy(
            ref.at[:, columns(h)],
            kv.at[OWN, h, pl.ds(which * TOK, TOK)],
            load_sem.at[which, h],
        )

    def begin(h, carry):
        load(0, k_ref, h).start()
        load(1, v_ref, h).start()
        return carry

    lax.fori_loop(0, heads, begin, 0)
    rows = (
        pltpu.make_async_copy(q_ref, q_buf, row_sem.at[0]),
        pltpu.make_async_copy(do_ref, do_buf, row_sem.at[1]),
    )
    for row in rows:
        row.start()

    offsets = (REACH, 3 - 2 * core, 4 - 4 * half, 1 + 2 * core, 4 * half)
    query_block = lax.broadcasted_iota(jnp.int32, (1, TOK), 1) // BLOCK
    for slot in range(SLOTS):
        group = here + offsets[slot] - REACH
        exists = ((group >= 0) & (group < tm_count)).astype(jnp.int32)
        for key_block in range(BLOCKS):
            frame, band = key_block // BANDS, key_block % BANDS
            row = jnp.zeros((1, TOK), jnp.int32)
            for at in range(BLOCKS):
                if slot == OWN and at == key_block:
                    listed = 1
                else:
                    cand = (offsets[slot] * FRAMES + frame) * 3 + band - at % BANDS + 1
                    listed = list_ref[at, cand] * exists
                row = jnp.where(query_block == at, listed, row)
            index = slot * BLOCKS + key_block
            bias_ref[index:index + 1, :] = jnp.where(row > 0, 0.0, -jnp.inf)

    @pl.when(~has_relay)
    def _():
        def clear(h, carry):
            kv[RELAY, h] = jnp.zeros((2 * TOK, HDIM), jnp.bfloat16)
            return carry

        lax.fori_loop(0, heads, clear, 0)

    @pl.when(same & ~has_relay)
    def _():
        def clear(h, carry):
            kv[EXTRA, h] = jnp.zeros((2 * TOK, HDIM), jnp.bfloat16)
            return carry

        lax.fori_loop(0, heads, clear, 0)

    pl.semaphore_wait(barrier, 2 + down.astype(jnp.int32) + up.astype(jnp.int32))

    def forward(slot_from, slot_to, h, device):
        return pltpu.make_async_remote_copy(
            src_ref=kv.at[slot_from, h],
            dst_ref=kv.at[slot_to, h],
            send_sem=fwd_send.at[slot_to - 1, h],
            recv_sem=fwd_recv.at[slot_to - 1, h],
            device_id={"tm": device},
            device_id_type=MESH,
        )

    def backward(slot, h, device):
        return pltpu.make_async_remote_copy(
            src_ref=back_out.at[slot - 1, h],
            dst_ref=back_in.at[slot - 1, h],
            send_sem=back_send.at[slot - 1, h],
            recv_sem=back_recv.at[slot - 1, h],
            device_id={"tm": device},
            device_id_type=MESH,
        )

    def store(which, h):
        src = dq_buf.at[h] if which == 0 else out_buf.at[h, pl.ds((which - 1) * TOK, TOK)]
        return pltpu.make_async_copy(
            src, (dq_ref, dk_ref, dv_ref)[which].at[:, columns(h)], store_sem.at[which, h]
        )

    def send_own(h):
        load(0, k_ref, h).wait()
        load(1, v_ref, h).wait()
        forward(OWN, PARTNER, h, partner).start()
        forward(OWN, SIB, h, sibling).start()

    def first(h, carry):
        send_own(h)
        return carry

    lax.fori_loop(0, min(AHEAD, heads), first, 0)

    for row in rows:
        row.wait()

    def pass_partner(h):
        forward(OWN, PARTNER, h, partner).wait_recv()

        @pl.when(has_target)
        def _():
            forward(PARTNER, RELAY, h, target).start()

        @pl.when(same)
        def _():
            forward(PARTNER, EXTRA, h, sibling).start()

    def pass_relay(h):
        @pl.when(has_relay)
        def _():
            forward(PARTNER, RELAY, h, target).wait_recv()

        @pl.when(has_relay & ~same)
        def _():
            forward(RELAY, EXTRA, h, sibling).start()

    def compute(h):
        forward(OWN, SIB, h, sibling).wait_recv()

        @pl.when(has_relay | ~same)
        def _():
            forward(PARTNER, EXTRA, h, sibling).wait_recv()

        query = q_buf[:, columns(h)]
        grad = do_buf[:, columns(h)]
        scores, probs = [], []
        top = None
        for slot in range(SLOTS):
            raw = lax.dot_general(
                kv[slot, h, 0:TOK, :], query, (((1,), (1,)), ((), ())),
                preferred_element_type=jnp.float32,
            )
            parts = [
                raw[b * BLOCK:(b + 1) * BLOCK] * scale2
                + bias_ref[slot * BLOCKS + b:slot * BLOCKS + b + 1, :]
                for b in range(BLOCKS)
            ]
            score = jnp.concatenate(parts, axis=0)
            scores.append(score)
            peak = jnp.max(score, axis=0, keepdims=True)
            top = peak if top is None else jnp.maximum(top, peak)
        total = jnp.zeros((1, TOK), jnp.float32)
        dot = jnp.zeros((1, TOK), jnp.float32)
        weights = []
        for slot in range(SLOTS):
            prob = lax.dot_general(
                kv[slot, h, TOK:2 * TOK, :], grad, (((1,), (1,)), ((), ())),
                preferred_element_type=jnp.float32,
            )
            weight = jnp.exp2(scores[slot] - top)
            total = total + jnp.sum(weight, axis=0, keepdims=True)
            dot = dot + jnp.sum(weight * prob, axis=0, keepdims=True)
            weights.append(weight)
            probs.append(prob)
        inverse = 1.0 / total
        delta = dot * inverse
        query_grad = jnp.zeros((TOK, HDIM), jnp.float32)
        for slot in range(SLOTS):
            weight = weights[slot] * inverse
            low = weight.astype(jnp.bfloat16)
            grad_score = (weight * (probs[slot] - delta)).astype(jnp.bfloat16)
            value_part = jnp.dot(low, grad, preferred_element_type=jnp.float32)
            key_part = jnp.dot(grad_score, query, preferred_element_type=jnp.float32) * scale
            query_grad = query_grad + lax.dot_general(
                grad_score, kv[slot, h, 0:TOK, :], (((0,), (0,)), ((), ())),
                preferred_element_type=jnp.float32,
            )
            if slot in (SIB, EXTRA):
                back_out[slot - 1, h, 0:TOK, :] = key_part.astype(jnp.bfloat16)
                back_out[slot - 1, h, TOK:2 * TOK, :] = value_part.astype(jnp.bfloat16)
            else:
                acc = {OWN: own_acc, PARTNER: partner_acc, RELAY: relay_acc}[slot]
                acc[h, 0:TOK, :] = key_part
                acc[h, TOK:2 * TOK, :] = value_part
        dq_buf[h] = (query_grad * scale).astype(jnp.bfloat16)
        store(0, h).start()

        backward(SIB, h, sibling).start()

        @pl.when(has_relay | ~same)
        def _():
            backward(EXTRA, h, sibling).start()

    def return_relay(h):
        @pl.when(same)
        def _():
            backward(EXTRA, h, sibling).wait_recv()
            partner_acc[h] = partner_acc[h] + back_in[EXTRA - 1, h].astype(jnp.float32)

        @pl.when(has_relay & ~same)
        def _():
            backward(EXTRA, h, sibling).wait_recv()
            relay_acc[h] = relay_acc[h] + back_in[EXTRA - 1, h].astype(jnp.float32)

        @pl.when(has_relay)
        def _():
            back_out[RELAY - 1, h] = relay_acc[h].astype(jnp.bfloat16)
            backward(RELAY, h, source).start()

    def return_partner(h):
        @pl.when(has_target)
        def _():
            backward(RELAY, h, source).wait_recv()
            partner_acc[h] = partner_acc[h] + back_in[RELAY - 1, h].astype(jnp.float32)

        back_out[PARTNER - 1, h] = partner_acc[h].astype(jnp.bfloat16)
        backward(PARTNER, h, partner).start()

    def finish(h):
        backward(SIB, h, sibling).wait_recv()
        backward(PARTNER, h, partner).wait_recv()
        done = (
            own_acc[h]
            + back_in[SIB - 1, h].astype(jnp.float32)
            + back_in[PARTNER - 1, h].astype(jnp.float32)
        ).astype(jnp.bfloat16)
        out_buf[h] = done
        store(1, h).start()
        store(2, h).start()

    stages = (
        (0, pass_partner), (1, pass_relay), (6, return_partner), (4, return_relay), (2, compute),
    )

    def step(at, carry):
        if AHEAD < heads:
            @pl.when(at + AHEAD < heads)
            def _():
                send_own(at + AHEAD)

        for lag, stage in stages:
            @pl.when((at >= lag) & (at < heads + lag))
            def _(stage=stage, lag=lag):
                stage(at - lag)

        return carry

    lax.fori_loop(0, heads + max(lag for lag, _ in stages), step, 0)

    def last(h, carry):
        finish(h)
        return carry

    lax.fori_loop(0, heads, last, 0)

    def drain(h, carry):
        for which in range(3):
            store(which, h).wait()
        forward(OWN, PARTNER, h, partner).wait_send()
        forward(OWN, SIB, h, sibling).wait_send()
        backward(SIB, h, sibling).wait_send()
        backward(PARTNER, h, partner).wait_send()

        @pl.when(has_target)
        def _():
            forward(PARTNER, RELAY, h, target).wait_send()

        @pl.when(has_relay)
        def _():
            backward(RELAY, h, source).wait_send()

        @pl.when(same | has_relay)
        def _():
            forward(PARTNER, EXTRA, h, sibling).wait_send()

        @pl.when(~same | has_relay)
        def _():
            backward(EXTRA, h, sibling).wait_send()

        return carry

    lax.fori_loop(0, heads, drain, 0)


def settle_kernel(*refs):
    for src, dst in zip(refs[:3], refs[3:]):
        dst[...] = src[...]


def local(tm_count, queries, keys, values, grad_out, block_list):
    heads = queries.shape[1] // HDIM
    out = jax.ShapeDtypeStruct(queries.shape, jnp.bfloat16)
    hbm = pl.BlockSpec(memory_space=pl.ANY)
    pair = (heads, 2 * TOK, HDIM)
    grads = pl.pallas_call(
        functools.partial(kernel, tm_count, heads),
        out_shape=(out,) * 3,
        in_specs=[hbm] * 4 + [pl.BlockSpec(memory_space=pltpu.SMEM)],
        out_specs=(hbm,) * 3,
        scratch_shapes=[
            pltpu.VMEM((SLOTS * BLOCKS, TOK), jnp.float32),
            pltpu.VMEM(queries.shape, jnp.bfloat16),
            pltpu.VMEM(queries.shape, jnp.bfloat16),
            pltpu.VMEM((heads, TOK, HDIM), jnp.bfloat16),
            pltpu.VMEM(pair, jnp.bfloat16),
            pltpu.VMEM((SLOTS,) + pair, jnp.bfloat16),
            pltpu.VMEM((SLOTS - 1,) + pair, jnp.bfloat16),
            pltpu.VMEM((SLOTS - 1,) + pair, jnp.bfloat16),
            pltpu.VMEM(pair, jnp.float32),
            pltpu.VMEM(pair, jnp.float32),
            pltpu.VMEM(pair, jnp.float32),
            pltpu.SemaphoreType.DMA((2,)),
            pltpu.SemaphoreType.DMA((2, heads)),
            pltpu.SemaphoreType.DMA((3, heads)),
            pltpu.SemaphoreType.DMA((SLOTS - 1, heads)),
            pltpu.SemaphoreType.DMA((SLOTS - 1, heads)),
            pltpu.SemaphoreType.DMA((SLOTS - 1, heads)),
            pltpu.SemaphoreType.DMA((SLOTS - 1, heads)),
        ],
        compiler_params=pltpu.CompilerParams(
            collective_id=0, has_side_effects=True, vmem_limit_bytes=56 * 2**20
        ),
    )(queries, keys, values, grad_out, block_list)
    rows = pl.BlockSpec((BLOCK, queries.shape[1]), lambda i: (i, 0))
    return pl.pallas_call(
        settle_kernel,
        out_shape=(out,) * 3,
        grid=(BLOCKS,),
        in_specs=[rows] * 3,
        out_specs=(rows,) * 3,
        compiler_params=pltpu.CompilerParams(vmem_limit_bytes=56 * 2**20),
    )(*grads)


def solution(mesh):
    placed = P(("group", "tm"), None)
    return jax.shard_map(
        functools.partial(local, mesh.shape["tm"]),
        mesh=mesh,
        in_specs=(placed,) * 5,
        out_specs=(placed,) * 3,
        check_vma=False,
    )
```
